32 devices in a mesh: groups: 2 (over x), wide: 16 (over z, y, core).
Axes of the slice: x: 2, y: 2, z: 4, core: 2. Of those that a mesh axis runs over, the one named last changes fastest.
Arguments:
- acts: bfloat16 [2, 512, 8192], P(None, 'groups', 'wide'), parts along dimension 1, may hold values from -6 to 6
- output_weight: bfloat16 [8192, 8192], P('wide'), may hold values from -0.0625 to 0.0625
- adapter_down_weight: bfloat16 [16, 8192, 64], P('wide'), may hold values from -0.0625 to 0.0625
- adapter_up_weight: bfloat16 [16, 64, 8192], P('wide'), may hold values from -0.75 to 0.75
- row_adapter_numbers: int32 [2, 512, 1], P(None, 'groups'), parts along dimension 1, may hold values from 0 to 15; in each aligned block of 256 rows (0 to 255, 256 to 511, ..., all dimensions but the last counted through in order) at most 48 rows name the same one
Outputs:
- projected: bfloat16 [2, 512, 8192], P(None, ('groups', 'wide')), parts along dimension 1
The draws below stay inside these ranges and needn't reach their ends.
There are 2 independent parts, one for each index of `groups`. The reference program is written for one: setup_inputs(seed, part) draws one part's arguments, and reference() takes and returns one part's arrays. A program takes and returns all parts, laid end to end along the dimension named above; an argument that names none is the same for every part. Nothing has to cross between parts.
Inputs may be any that keep to these rules, and one draw needn't show every extreme that they name: `row_adapter_numbers`: in each step at most 48 rows name the same adapter, and in some step one adapter is named by exactly 48 rows.
All inputs are finite; a program needn't handle non-finite values.
Results may differ from the reference program's by a relative error of at most 0.0041.
Values may be sent and summed in bfloat16 or wider, within the bound.
A program may use at most 128 MiB of HBM per device.

```python
import math
import jax
import jax.numpy as jnp
import numpy as np
from jax import lax

MODEL_WIDTH = 8192
ADAPTER_RANK = 64
DECODE_STEPS = 2
DECODE_ROWS = 256
ADAPTER_COUNT = 16
CAP = 48


def level_of(own_key, extent, shards, smallest, largest):
    def one(position, shards_of):
        heights = jax.random.uniform(jax.random.fold_in(jax.random.fold_in(own_key, 6), position), (shards_of,), jnp.float32, smallest / len(shards), largest / len(shards))
        return jnp.repeat(jnp.exp(heights), extent[position] // shards_of).reshape((-1,) + (1,) * (len(extent) - position - 1))

    loudness = one(*shards[0])
    for cut in shards[1:]:
        loudness = loudness * one(*cut)
    return loudness


def assign_block(rng, own, number, rows, number_of, top, reach, lean):
    ranking = jax.random.permutation(rng, number_of)
    heavy_load, usual = portions_of(number_of, rows * top, reach, lean, True), portions_of(number_of, rows * top, reach, lean, False)
    places = jnp.arange(number_of)

    def named(lengths, rotation):
        used = int((lengths > 0).sum())
        fixed = max(1, used // 4)
        moved = fixed + (places - fixed + rotation * (used - fixed)) % max(1, number_of - fixed)
        return jnp.zeros((number_of,), jnp.int32).at[ranking[jnp.where(places < fixed, places, moved)]].set(jnp.asarray(lengths, jnp.int32))

    lengths = jnp.where(number % 4 == 0, named(heavy_load, number // 4), named(usual, number - number // 4 - 1))
    mixed = jax.random.permutation(jax.random.fold_in(own, 3), number_of)
    donor, sink = mixed[0:number_of // 2 * 2:2], mixed[1:number_of // 2 * 2:2]
    margin = jnp.minimum(lengths[donor] - 1, reach - lengths[sink]) // 2
    margin = jnp.where((donor == ranking[0]) | (sink == ranking[0]) | (lengths[sink] == 0), 0, jnp.maximum(margin, 0))
    moved = jax.random.randint(jax.random.fold_in(own, 4), (number_of // 2,), 0, 1 << 20) % (margin + 1)
    lengths = lengths.at[donor].add(-moved).at[sink].add(moved)
    labels = jnp.searchsorted(jnp.cumsum(lengths), jnp.arange(rows * top), side="right").astype(jnp.int32)
    table = labels.reshape(top, rows).T
    table = table[jax.random.permutation(jax.random.fold_in(own, 1), rows)]
    rotation = jax.random.randint(jax.random.fold_in(own, 2), (rows, 1), 0, top)
    return jnp.take_along_axis(table, (jnp.arange(top)[None, :] + rotation) % top, axis=1)


def portions_of(number_of, total, limit, skew, full):
    portions = [(1 << 20) // math.isqrt(standing ** skew) + 1 for standing in range(1, number_of + 1)]
    largest = limit if full else min(limit, max(-(-total // number_of), total * portions[0] // sum(portions)))
    least = 1 if total - largest >= number_of - 1 else 0
    counts, rest = [largest] + [least] * (number_of - 1), total - largest - least * (number_of - 1)
    while rest > 0:
        movable = [i for i in range(1, number_of) if counts[i] < largest] or [i for i in range(1, number_of) if counts[i] < limit]
        pool, budget = sum([portions[i] for i in movable]), rest
        for i in movable:
            addition = min(limit - counts[i], max(1, budget * portions[i] // pool), rest)
            counts[i] = counts[i] + addition
            rest = rest - addition
    return np.array(counts)


def scatter_about(own_key, dims, width, most, cuts=(), kind=jnp.bfloat16):
    drawn = width * jax.random.normal(own_key, dims, jnp.float32)
    if cuts:
        drawn = drawn * level_of(own_key, dims, cuts, -0.22, 0.18)
    return jnp.clip(drawn, -most, most).astype(kind)


def setup_inputs(seed: int = 0, part: int = 0) -> dict:
    streams_of = jax.random.split(jax.random.key(seed), 6)
    part_splits = jax.random.split(jax.random.fold_in(streams_of[5], part), 6)
    acts = scatter_about(part_splits[0], (DECODE_STEPS, DECODE_ROWS, MODEL_WIDTH), 1.0, 6.0, ((2, 16),))
    output_weight = scatter_about(streams_of[1], (MODEL_WIDTH, MODEL_WIDTH), MODEL_WIDTH ** -0.5, 0.0625, ((0, 16),))
    adapter_down_weight = scatter_about(streams_of[2], (ADAPTER_COUNT, MODEL_WIDTH, ADAPTER_RANK), MODEL_WIDTH ** -0.5, 0.0625, ((0, 16),))
    adapter_up_weight = scatter_about(streams_of[3], (ADAPTER_COUNT, ADAPTER_RANK, MODEL_WIDTH), ADAPTER_RANK ** -0.5, 0.75, ((0, 16),))
    row_adapter_numbers_keys = jax.random.split(jax.random.fold_in(part_splits[4], 1), DECODE_STEPS * DECODE_ROWS // DECODE_ROWS)
    row_adapter_numbers_turns = jax.random.permutation(jax.random.fold_in(part_splits[4], 3), DECODE_STEPS * DECODE_ROWS // DECODE_ROWS)
    row_adapter_numbers = jax.vmap(lambda own, number: assign_block(jax.random.fold_in(part_splits[4], 2), own, number, DECODE_ROWS, ADAPTER_COUNT, 1, CAP, 2))(row_adapter_numbers_keys, row_adapter_numbers_turns).reshape((DECODE_STEPS, DECODE_ROWS, 1))
    return dict(acts=acts, output_weight=output_weight, adapter_down_weight=adapter_down_weight, adapter_up_weight=adapter_up_weight, row_adapter_numbers=row_adapter_numbers)


def reference(acts, output_weight, adapter_down_weight, adapter_up_weight, row_adapter_numbers):
    flat_rows = acts.reshape(DECODE_STEPS * DECODE_ROWS, MODEL_WIDTH)
    row_ids = row_adapter_numbers.reshape(DECODE_STEPS * DECODE_ROWS).astype(jnp.int32)

    def shrink_step(adapter_position, summed):
        down_weight_block = lax.dynamic_index_in_dim(adapter_down_weight, adapter_position, 0, keepdims=False)
        part_rows = jnp.dot(flat_rows, down_weight_block, preferred_element_type=jnp.float32)
        return summed + jnp.where((row_ids == adapter_position)[:, None], part_rows, jnp.zeros_like(part_rows))

    shrunk = lax.fori_loop(0, ADAPTER_COUNT, shrink_step, jnp.zeros((DECODE_STEPS * DECODE_ROWS, ADAPTER_RANK), jnp.float32))
    low_rows = shrunk.astype(jnp.bfloat16)

    def expand_decode_step(adapter_position, summed):
        up_weight_block = lax.dynamic_index_in_dim(adapter_up_weight, adapter_position, 0, keepdims=False)
        chosen = jnp.where((row_ids == adapter_position)[:, None], low_rows, jnp.zeros_like(low_rows))
        return summed + jnp.dot(chosen, up_weight_block, preferred_element_type=jnp.float32)

    adapter_delta = lax.fori_loop(0, ADAPTER_COUNT, expand_decode_step, jnp.zeros((DECODE_STEPS * DECODE_ROWS, MODEL_WIDTH), jnp.float32))
    base_output_rows = jnp.dot(flat_rows, output_weight, preferred_element_type=jnp.float32)
    return (base_output_rows + adapter_delta).astype(jnp.bfloat16).reshape(DECODE_STEPS, DECODE_ROWS, MODEL_WIDTH)
```

```python
import functools

import jax
import jax.numpy as jnp
from jax import lax
from jax.experimental import pallas as pl
from jax.experimental.pallas import tpu as pltpu
from jax.sharding import PartitionSpec as P

CHUNKS = 8


def kernel(
    devices,
    stages,
    ids_ref,
    acts_ref,
    weight_ref,
    down_ref,
    up_ref,
    out_ref,
    acts_sib,
    weight_own,
    weight_sib,
    down_all,
    up_pair,
    total,
    low_part,
    low_got,
    low_all,
    low_mine,
    swap,
    *rest,
):
    sends, gots = rest[:stages], rest[stages : 2 * stages]
    (
        acts_sem,
        up_sem,
        weight_send,
        weight_recv,
        weight_local,
        down_send,
        down_recv,
        low_send,
        low_recv,
        all_send,
        all_recv,
        half_send,
        half_recv,
        swap_send,
        swap_recv,
    ) = rest[2 * stages :]
    me = lax.axis_index("wide")
    core = lax.rem(me, 2)
    chip = me // 2
    sibling = me + 1 - 2 * core
    rows, feats = acts_ref.shape
    rank = up_ref.shape[0]
    chunks, _, width = weight_own.shape
    half_columns = chunks * width
    block = rows // devices

    barrier = pltpu.get_barrier_semaphore()

    def greet(i, carry):
        pl.semaphore_signal(
            barrier,
            inc=1,
            device_id={"wide": lax.rem(me + i, devices)},
            device_id_type=pl.DeviceIdType.MESH,
        )
        return carry

    lax.fori_loop(1, devices, greet, 0)
    pl.semaphore_wait(barrier, devices - 1)

    def remote(src, dst, send, recv, to):
        return pltpu.make_async_remote_copy(
            src_ref=src,
            dst_ref=dst,
            send_sem=send,
            recv_sem=recv,
            device_id={"wide": to},
            device_id_type=pl.DeviceIdType.MESH,
        )

    def down_copy(to, owner):
        return remote(
            down_ref.at[to],
            down_all.at[pl.ds(pl.multiple_of(owner * rank, rank), rank)],
            down_send.at[to],
            down_recv.at[owner],
            to,
        )

    def low_copy(to, owner):
        return remote(
            low_part.at[to], low_got.at[owner], low_send.at[to], low_recv.at[owner], to
        )

    def all_copy(to, owner):
        return remote(
            low_all.at[owner], low_all.at[owner], all_send.at[to], all_recv.at[owner], to
        )

    def weight_copy(k):
        start = pl.multiple_of((1 - core) * half_columns + k * width, width)
        return remote(
            weight_ref.at[:, pl.ds(start, width)],
            weight_sib.at[k],
            weight_send.at[k],
            weight_recv.at[k],
            sibling,
        )

    def weight_fetch(k):
        start = pl.multiple_of(core * half_columns + k * width, width)
        return pltpu.make_async_copy(
            weight_ref.at[:, pl.ds(start, width)], weight_own.at[k], weight_local.at[k]
        )

    def each_peer(action):
        def one(i, carry):
            action(lax.rem(me + i, devices))
            return carry

        lax.fori_loop(1, devices, one, 0)

    def each_chunk(action):
        def one(k, carry):
            action(k)
            return carry

        lax.fori_loop(0, chunks, one, 0)

    own_rank = pl.ds(pl.multiple_of(core * rank, rank), rank)
    acts_copy = remote(acts_ref, acts_sib, acts_sem.at[0], acts_sem.at[1], sibling)
    up_copy = remote(
        up_ref.at[:, pl.ds(pl.multiple_of((1 - core) * half_columns, width), half_columns)],
        up_pair.at[own_rank],
        up_sem.at[0],
        up_sem.at[1],
        sibling,
    )
    up_fetch = pltpu.make_async_copy(
        up_ref.at[:, pl.ds(pl.multiple_of(core * half_columns, width), half_columns)],
        up_pair.at[own_rank],
        up_sem.at[2],
    )
    down_fetch = pltpu.make_async_copy(
        down_ref.at[me],
        down_all.at[pl.ds(pl.multiple_of(me * rank, rank), rank)],
        down_send.at[me],
    )
    each_peer(lambda peer: down_copy(peer, me).start())
    down_fetch.start()
    acts_copy.start()

    def load(k):
        weight_fetch(k).start()
        weight_copy(k).start()

    each_chunk(load)
    up_copy.start()
    up_fetch.start()

    acts_copy.wait_recv()

    def base(k):
        weight_fetch(k).wait()
        weight_copy(k).wait_recv()
        total[k] = jnp.dot(
            acts_ref[...], weight_own[k], preferred_element_type=jnp.float32
        ) + jnp.dot(acts_sib[...], weight_sib[k], preferred_element_type=jnp.float32)

    each_chunk(base)

    down_fetch.wait()
    each_peer(lambda peer: down_copy(me, peer).wait_recv())
    odd = (lax.broadcasted_iota(jnp.int32, (rows, 2 * rank), 1) >= rank).astype(jnp.int32)
    number = ids_ref[...] - odd
    low_part[...] = jnp.zeros_like(low_part)

    def shrink(j, carry):
        pair = down_all[pl.ds(pl.multiple_of(j * 2 * rank, 2 * rank), 2 * rank)]
        part = lax.dot_general(
            acts_ref[...], pair, (((1,), (1,)), ((), ())), preferred_element_type=jnp.float32
        )
        part = jnp.where(number == 2 * j, part, 0.0)
        low_part[...] += part.reshape(devices, block, 2 * rank)
        return carry

    lax.fori_loop(0, devices // 2, shrink, 0)
    each_peer(lambda peer: low_copy(peer, me).start())

    def gather(i, value):
        peer = lax.rem(me + i, devices)
        low_copy(me, peer).wait_recv()
        return value + low_got[peer]

    low_all[me] = lax.fori_loop(1, devices, gather, low_part[me]).astype(jnp.bfloat16)
    each_peer(lambda peer: all_copy(peer, me).start())
    each_peer(lambda peer: all_copy(me, peer).wait_recv())
    everything = low_all[...].astype(jnp.float32).reshape(rows, 2 * rank)
    low_mine[...] = jnp.where(number == 2 * chip, everything, 0.0).astype(jnp.bfloat16)
    up_fetch.wait()
    up_copy.wait_recv()

    bits = [lax.rem(chip // 2**s, 2) for s in range(stages)]
    partners = [me + 2 ** (s + 1) * (1 - 2 * bits[s]) for s in range(stages)]

    def half_copy(s, k):
        return remote(
            sends[s].at[k],
            gots[s].at[k],
            half_send.at[s * chunks + k],
            half_recv.at[s * chunks + k],
            partners[s],
        )

    half = rows // 2

    def delta(k, start):
        return jnp.dot(
            low_mine[pl.ds(start, half)],
            up_pair[:, pl.ds(pl.multiple_of(k * width, width), width)],
            preferred_element_type=jnp.float32,
        )

    away = pl.multiple_of((1 - bits[0]) * half, half)
    kept = pl.multiple_of(bits[0] * half, half)

    def first(k):
        sends[0][k] = (total[k, pl.ds(away, half)] + delta(k, away)).astype(jnp.bfloat16)
        half_copy(0, k).start()

    def second(k):
        total[k, pl.ds(kept, half)] += delta(k, kept)

    each_chunk(first)
    each_chunk(second)

    def swap_copy(k):
        return remote(
            swap.at[k],
            out_ref.at[core * chunks + k],
            swap_send.at[k],
            swap_recv.at[k],
            sibling,
        )

    def finish(s, k, offset, size):
        half_copy(s, k).wait_recv()
        small = size // 2
        last = s == stages - 1
        bit = core if last else bits[s + 1]
        there = pl.multiple_of((1 - bit) * small, small)
        here = pl.multiple_of(bit * small, small)
        away = total[k, pl.ds(pl.multiple_of(offset + there, small), small)] + gots[s][
            k, pl.ds(there, small)
        ].astype(jnp.float32)
        if last:
            swap[k] = away.astype(jnp.bfloat16)
            swap_copy(k).start()
        else:
            sends[s + 1][k] = away.astype(jnp.bfloat16)
            half_copy(s + 1, k).start()
        mine = pl.ds(pl.multiple_of(offset + here, small), small)
        value = total[k, mine] + gots[s][k, pl.ds(here, small)].astype(jnp.float32)
        if last:
            out_ref[core * chunks + k] = value.astype(jnp.bfloat16)
        else:
            total[k, mine] = value

    offsets, sizes = [kept], [half]
    for s in range(1, stages):
        sizes.append(sizes[-1] // 2)
        offsets.append(offsets[-1] + bits[s] * sizes[-1])

    def step(t, carry):
        for s in range(stages):

            @pl.when((t >= s) & (t - s < chunks))
            def _():
                finish(s, t - s, offsets[s], sizes[s])

        return carry

    lax.fori_loop(0, chunks + stages - 1, step, 0)

    other = 1 - core

    def close(k):
        remote(
            swap.at[k],
            out_ref.at[other * chunks + k],
            swap_send.at[k],
            swap_recv.at[k],
            sibling,
        ).wait_recv()
        swap_copy(k).wait_send()
        weight_copy(k).wait_send()
        for s in range(stages):
            half_copy(s, k).wait_send()

    each_chunk(close)

    def close_peer(peer):
        down_copy(peer, me).wait_send()
        low_copy(peer, me).wait_send()
        all_copy(peer, me).wait_send()

    each_peer(close_peer)
    acts_copy.wait_send()
    up_copy.wait_send()


def shards(devices, acts, weight, down, up, numbers):
    steps, rows, feats = acts.shape
    rank, columns = up.shape[1:]
    chips = devices // 2
    stages = chips.bit_length() - 1
    block = rows // devices
    total_rows = steps * rows
    width = columns // 2 // CHUNKS
    order = tuple(range(stages, 0, -1)) + (stages + 1, 0, stages + 2, stages + 3)

    def arranged(array):
        array = array.reshape((steps,) + (2,) * stages + (2, block, array.shape[-1]))
        return array.transpose(order).reshape(total_rows, array.shape[-1])

    down = down.reshape(devices, feats, rank).swapaxes(1, 2)
    bf16, f32 = jnp.bfloat16, jnp.float32
    low_block = (devices, total_rows // devices, 2 * rank)
    halves = [(CHUNKS, total_rows >> (s + 1), width) for s in range(stages)]
    dma = pltpu.SemaphoreType.DMA
    out = pl.pallas_call(
        functools.partial(kernel, devices, stages),
        out_shape=jax.ShapeDtypeStruct((2 * CHUNKS, steps * block, width), bf16),
        in_specs=[
            pl.BlockSpec(memory_space=pltpu.VMEM),
            pl.BlockSpec(memory_space=pltpu.VMEM),
            pl.BlockSpec(memory_space=pl.ANY),
            pl.BlockSpec(memory_space=pl.ANY),
            pl.BlockSpec(memory_space=pl.ANY),
        ],
        out_specs=pl.BlockSpec(memory_space=pltpu.VMEM),
        scratch_shapes=[
            pltpu.VMEM((total_rows, feats), bf16),
            pltpu.VMEM((CHUNKS, feats, width), bf16),
            pltpu.VMEM((CHUNKS, feats, width), bf16),
            pltpu.VMEM((devices * rank, feats), bf16),
            pltpu.VMEM((2 * rank, columns // 2), bf16),
            pltpu.VMEM((CHUNKS, total_rows, width), f32),
            pltpu.VMEM(low_block, f32),
            pltpu.VMEM(low_block, f32),
            pltpu.VMEM(low_block, bf16),
            pltpu.VMEM((total_rows, 2 * rank), bf16),
            pltpu.VMEM((CHUNKS, steps * block, width), bf16),
        ]
        + [pltpu.VMEM(shape, bf16) for shape in halves]
        + [pltpu.VMEM(shape, bf16) for shape in halves]
        + [dma((2,)), dma((3,))]
        + [dma((CHUNKS,))] * 3
        + [dma((devices,))] * 6
        + [dma((stages * CHUNKS,))] * 2
        + [dma((CHUNKS,))] * 2,
        compiler_params=pltpu.CompilerParams(
            collective_id=0, has_side_effects=True, vmem_limit_bytes=58 * 1024 * 1024
        ),
    )(arranged(numbers), arranged(acts), weight, down, up.reshape(rank, columns))
    out = out.reshape(2 * CHUNKS, steps, block, width).transpose(1, 2, 0, 3)
    return out.reshape(steps, block, columns)


def solution(mesh):
    in_specs = (
        P(None, "groups", "wide"),
        P("wide", None),
        P("wide", None, None),
        P("wide", None, None),
        P(None, "groups", None),
    )
    out_specs = P(None, ("groups", "wide"), None)
    return jax.shard_map(
        functools.partial(shards, mesh.shape["wide"]),
        mesh=mesh,
        in_specs=in_specs,
        out_specs=out_specs,
        check_vma=False,
    )
```

```python
import functools

import jax
import jax.numpy as jnp
from jax import lax
from jax.experimental import pallas as pl
from jax.experimental.pallas import tpu as pltpu
from jax.sharding import PartitionSpec as P

CHUNKS = 8
EARLY = 3


def kernel(
    devices,
    groups,
    stages,
    ids_ref,
    acts_ref,
    weight_ref,
    down_ref,
    up_ref,
    out_ref,
    acts_sib,
    weight_own,
    weight_sib,
    down_all,
    up_pair,
    up_far,
    total,
    low_sum,
    low_part,
    low_got,
    low_all,
    low_mine,
    low_far,
    swap,
    *rest,
):
    sends, gots = rest[:stages], rest[stages : 2 * stages]
    (
        acts_sem,
        up_sem,
        far_sem,
        weight_send,
        weight_recv,
        weight_local,
        down_send,
        down_recv,
        pass_send,
        low_send,
        low_recv,
        all_send,
        all_recv,
        half_send,
        half_recv,
        swap_send,
        swap_recv,
    ) = rest[2 * stages :]
    me = lax.axis_index("wide")
    group = lax.axis_index("groups")
    core = lax.rem(me, 2)
    chip = me // 2
    sibling = me + 1 - 2 * core
    rows, feats = acts_ref.shape
    rank = up_ref.shape[0]
    chunks, _, width = weight_own.shape
    half_columns = chunks * width
    block = rows // devices

    barrier = pltpu.get_barrier_semaphore()

    def greet(i, carry):
        pl.semaphore_signal(
            barrier,
            inc=1,
            device_id={"wide": lax.rem(me + i, devices)},
            device_id_type=pl.DeviceIdType.MESH,
        )
        return carry

    lax.fori_loop(1, devices, greet, 0)
    for q in range(1, groups):
        pl.semaphore_signal(
            barrier,
            inc=1,
            device_id={"groups": lax.rem(group + q, groups), "wide": me},
            device_id_type=pl.DeviceIdType.MESH,
        )
    pl.semaphore_wait(barrier, devices + groups - 2)

    def remote(src, dst, send, recv, to):
        return pltpu.make_async_remote_copy(
            src_ref=src,
            dst_ref=dst,
            send_sem=send,
            recv_sem=recv,
            device_id={"wide": to},
            device_id_type=pl.DeviceIdType.MESH,
        )

    def down_copy(to, owner):
        return remote(
            down_ref.at[to],
            down_all.at[pl.ds(pl.multiple_of(owner * rank, rank), rank)],
            down_send.at[to],
            down_recv.at[owner],
            to,
        )

    def pass_copy(owner, q):
        piece = down_all.at[pl.ds(pl.multiple_of(owner * rank, rank), rank)]
        return pltpu.make_async_remote_copy(
            src_ref=piece,
            dst_ref=piece,
            send_sem=pass_send.at[owner * groups + q],
            recv_sem=down_recv.at[owner],
            device_id={"groups": lax.rem(group + q, groups), "wide": me},
            device_id_type=pl.DeviceIdType.MESH,
        )

    def low_copy(to, owner):
        return remote(
            low_part.at[to], low_got.at[owner], low_send.at[to], low_recv.at[owner], to
        )

    def all_copy(to, owner):
        return remote(
            low_all.at[owner], low_all.at[owner], all_send.at[to], all_recv.at[owner], to
        )

    def weight_copy(k):
        start = pl.multiple_of((1 - core) * half_columns + k * width, width)
        return remote(
            weight_ref.at[:, pl.ds(start, width)],
            weight_sib.at[k],
            weight_send.at[k],
            weight_recv.at[k],
            sibling,
        )

    def weight_fetch(k):
        start = pl.multiple_of(core * half_columns + k * width, width)
        return pltpu.make_async_copy(
            weight_ref.at[:, pl.ds(start, width)], weight_own.at[k], weight_local.at[k]
        )

    def each_peer(action):
        def one(i, carry):
            action(lax.rem(me + i, devices))
            return carry

        lax.fori_loop(1, devices, one, 0)

    def each_chunk(action, first=0, end=None):
        def one(k, carry):
            action(k)
            return carry

        lax.fori_loop(first, chunks if end is None else end, one, 0)

    bits = [lax.rem(chip // 2**s, 2) for s in range(stages)]
    partners = [me + 2 ** (s + 1) * (1 - 2 * bits[s]) for s in range(stages)]

    def half_copy(s, k):
        return remote(
            sends[s].at[k],
            gots[s].at[k],
            half_send.at[s * chunks + k],
            half_recv.at[s * chunks + k],
            partners[s],
        )

    half = rows // 2
    away = pl.multiple_of((1 - bits[0]) * half, half)
    kept = pl.multiple_of(bits[0] * half, half)
    early_columns = EARLY * width

    def fetched(peer):
        return lax.rem(me + peer, groups) == group

    own_rank = pl.ds(pl.multiple_of(core * rank, rank), rank)
    acts_copy = remote(acts_ref, acts_sib, acts_sem.at[0], acts_sem.at[1], sibling)
    up_copy = remote(
        up_ref.at[:, pl.ds(pl.multiple_of((1 - core) * half_columns, width), half_columns)],
        up_pair.at[own_rank],
        up_sem.at[0],
        up_sem.at[1],
        sibling,
    )
    up_fetch = pltpu.make_async_copy(
        up_ref.at[:, pl.ds(pl.multiple_of(core * half_columns, width), half_columns)],
        up_pair.at[own_rank],
        up_sem.at[2],
    )
    down_fetch = pltpu.make_async_copy(
        down_ref.at[me],
        down_all.at[pl.ds(pl.multiple_of(me * rank, rank), rank)],
        down_send.at[me],
    )
    each_peer(lambda peer: pl.when(fetched(peer))(lambda: down_copy(peer, me).start()))
    down_fetch.start()
    acts_copy.start()

    def load(k):
        weight_fetch(k).start()
        weight_copy(k).start()

    each_chunk(load)
    up_copy.start()
    up_fetch.start()

    acts_copy.wait_recv()

    def base(k):
        weight_fetch(k).wait()
        weight_copy(k).wait_recv()
        total[k] = jnp.dot(
            acts_ref[...], weight_own[k], preferred_element_type=jnp.float32
        ) + jnp.dot(acts_sib[...], weight_sib[k], preferred_element_type=jnp.float32)

    def base_early(k):
        base(k)
        sends[0][k] = total[k, pl.ds(away, half)].astype(jnp.bfloat16)
        half_copy(0, k).start()

    far_copy = remote(
        up_pair.at[:, pl.ds(0, early_columns)], up_far, far_sem.at[0], far_sem.at[1], partners[0]
    )
    each_chunk(base_early, 0, EARLY)
    up_fetch.wait()
    up_copy.wait_recv()
    far_copy.start()
    each_chunk(base, EARLY)

    down_fetch.wait()

    def arrive(peer):
        @pl.when(fetched(peer))
        def _():
            down_copy(me, peer).wait_recv()
            for q in range(1, groups):
                pass_copy(peer, q).start()

    def passed(peer):
        @pl.when(jnp.logical_not(fetched(peer)))
        def _():
            down_copy(me, peer).wait_recv()

    each_peer(arrive)
    each_peer(passed)
    odd = (lax.broadcasted_iota(jnp.int32, (rows, 2 * rank), 1) >= rank).astype(jnp.int32)
    number = ids_ref[...] - odd
    low_sum[...] = jnp.zeros_like(low_sum)

    def shrink(j, carry):
        pair = down_all[pl.ds(pl.multiple_of(j * 2 * rank, 2 * rank), 2 * rank)]
        part = lax.dot_general(
            acts_ref[...], pair, (((1,), (1,)), ((), ())), preferred_element_type=jnp.float32
        )
        low_sum[...] += jnp.where(number == 2 * j, part, 0.0)
        return carry

    lax.fori_loop(0, devices // 2, shrink, 0)
    pairs = rows // 2
    left = lax.broadcasted_iota(jnp.int32, (devices, block // 2, 2 * rank), 2) < rank
    both = low_sum[...] + pltpu.roll(low_sum[...], rank, 1)
    both = both.reshape(devices, 2, block // 2, 2 * rank)
    low_part[...] = jnp.where(left, both[:, 0], both[:, 1])
    each_peer(lambda peer: low_copy(peer, me).start())

    def gather(i, value):
        peer = lax.rem(me + i, devices)
        low_copy(me, peer).wait_recv()
        return value + low_got[peer]

    low_all[me] = lax.fori_loop(1, devices, gather, low_part[me]).astype(jnp.bfloat16)
    each_peer(lambda peer: all_copy(peer, me).start())
    each_peer(lambda peer: all_copy(me, peer).wait_recv())
    packed = low_all[...].astype(jnp.float32)
    turned = pltpu.roll(packed.reshape(pairs, 2 * rank), rank, 1).reshape(packed.shape)
    upper, lower = jnp.where(left, packed, turned), jnp.where(left, turned, packed)
    everything = jnp.stack([upper, lower], axis=1).reshape(rows, 2 * rank)
    low_mine[...] = jnp.where(number == 2 * chip, everything, 0.0).astype(jnp.bfloat16)
    low_far[...] = jnp.where(number == 2 * (partners[0] // 2), everything, 0.0).astype(
        jnp.bfloat16
    )

    def delta(k, start):
        return jnp.dot(
            low_mine[pl.ds(start, half)],
            up_pair[:, pl.ds(pl.multiple_of(k * width, width), width)],
            preferred_element_type=jnp.float32,
        )

    def first(k):
        sends[0][k] = (total[k, pl.ds(away, half)] + delta(k, away)).astype(jnp.bfloat16)
        half_copy(0, k).start()

    def second(k):
        total[k, pl.ds(kept, half)] += delta(k, kept)

    def second_far(k):
        total[k, pl.ds(kept, half)] += jnp.dot(
            low_far[pl.ds(kept, half)],
            up_far[:, pl.ds(pl.multiple_of(k * width, width), width)],
            preferred_element_type=jnp.float32,
        )

    each_chunk(first, EARLY)
    far_copy.wait_recv()

    def swap_copy(k):
        return remote(
            swap.at[k],
            out_ref.at[core * chunks + k],
            swap_send.at[k],
            swap_recv.at[k],
            sibling,
        )

    def finish(s, k, offset, size):
        half_copy(s, k).wait_recv()
        small = size // 2
        last = s == stages - 1
        bit = core if last else bits[s + 1]
        there = pl.multiple_of((1 - bit) * small, small)
        here = pl.multiple_of(bit * small, small)
        away = total[k, pl.ds(pl.multiple_of(offset + there, small), small)] + gots[s][
            k, pl.ds(there, small)
        ].astype(jnp.float32)
        if last:
            swap[k] = away.astype(jnp.bfloat16)
            swap_copy(k).start()
        else:
            sends[s + 1][k] = away.astype(jnp.bfloat16)
            half_copy(s + 1, k).start()
        mine = pl.ds(pl.multiple_of(offset + here, small), small)
        value = total[k, mine] + gots[s][k, pl.ds(here, small)].astype(jnp.float32)
        if last:
            out_ref[core * chunks + k] = value.astype(jnp.bfloat16)
        else:
            total[k, mine] = value

    offsets, sizes = [kept], [half]
    for s in range(1, stages):
        sizes.append(sizes[-1] // 2)
        offsets.append(offsets[-1] + bits[s] * sizes[-1])

    def step(t, carry):
        pl.when(t < chunks)(lambda: second(t))
        pl.when(t < EARLY)(lambda: second_far(t))
        for s in range(stages):

            @pl.when((t >= s) & (t - s < chunks))
            def _():
                finish(s, t - s, offsets[s], sizes[s])

        return carry

    lax.fori_loop(0, chunks + stages - 1, step, 0)

    other = 1 - core

    def close(k):
        remote(
            swap.at[k],
            out_ref.at[other * chunks + k],
            swap_send.at[k],
            swap_recv.at[k],
            sibling,
        ).wait_recv()
        swap_copy(k).wait_send()
        weight_copy(k).wait_send()
        for s in range(stages):
            half_copy(s, k).wait_send()

    each_chunk(close)

    def close_peer(peer):
        @pl.when(fetched(peer))
        def _():
            down_copy(peer, me).wait_send()
            for q in range(1, groups):
                pass_copy(peer, q).wait_send()

        low_copy(peer, me).wait_send()
        all_copy(peer, me).wait_send()

    each_peer(close_peer)
    acts_copy.wait_send()
    up_copy.wait_send()
    far_copy.wait_send()


def shards(devices, groups, acts, weight, down, up, numbers):
    steps, rows, feats = acts.shape
    rank, columns = up.shape[1:]
    chips = devices // 2
    stages = chips.bit_length() - 1
    block = rows // devices
    total_rows = steps * rows
    width = columns // 2 // CHUNKS
    order = tuple(range(stages, 0, -1)) + (stages + 1, 0, stages + 2, stages + 3)

    def arranged(array):
        array = array.reshape((steps,) + (2,) * stages + (2, block, array.shape[-1]))
        return array.transpose(order).reshape(total_rows, array.shape[-1])

    down = down.reshape(devices, feats, rank).swapaxes(1, 2)
    bf16, f32 = jnp.bfloat16, jnp.float32
    low_block = (devices, total_rows // devices // 2, 2 * rank)
    halves = [(CHUNKS, total_rows >> (s + 1), width) for s in range(stages)]
    dma = pltpu.SemaphoreType.DMA
    out = pl.pallas_call(
        functools.partial(kernel, devices, groups, stages),
        out_shape=jax.ShapeDtypeStruct((2 * CHUNKS, steps * block, width), bf16),
        in_specs=[
            pl.BlockSpec(memory_space=pltpu.VMEM),
            pl.BlockSpec(memory_space=pltpu.VMEM),
            pl.BlockSpec(memory_space=pl.ANY),
            pl.BlockSpec(memory_space=pl.ANY),
            pl.BlockSpec(memory_space=pl.ANY),
        ],
        out_specs=pl.BlockSpec(memory_space=pltpu.VMEM),
        scratch_shapes=[
            pltpu.VMEM((total_rows, feats), bf16),
            pltpu.VMEM((CHUNKS, feats, width), bf16),
            pltpu.VMEM((CHUNKS, feats, width), bf16),
            pltpu.VMEM((devices * rank, feats), bf16),
            pltpu.VMEM((2 * rank, columns // 2), bf16),
            pltpu.VMEM((2 * rank, EARLY * width), bf16),
            pltpu.VMEM((CHUNKS, total_rows, width), f32),
            pltpu.VMEM((total_rows, 2 * rank), f32),
            pltpu.VMEM(low_block, f32),
            pltpu.VMEM(low_block, f32),
            pltpu.VMEM(low_block, bf16),
            pltpu.VMEM((total_rows, 2 * rank), bf16),
            pltpu.VMEM((total_rows, 2 * rank), bf16),
            pltpu.VMEM((CHUNKS, steps * block, width), bf16),
        ]
        + [pltpu.VMEM(shape, bf16) for shape in halves]
        + [pltpu.VMEM(shape, bf16) for shape in halves]
        + [dma((2,)), dma((3,)), dma((2,))]
        + [dma((CHUNKS,))] * 3
        + [dma((devices,))] * 2
        + [dma((devices * groups,))]
        + [dma((devices,))] * 4
        + [dma((stages * CHUNKS,))] * 2
        + [dma((CHUNKS,))] * 2,
        compiler_params=pltpu.CompilerParams(
            collective_id=0, has_side_effects=True, vmem_limit_bytes=58 * 1024 * 1024
        ),
    )(arranged(numbers), arranged(acts), weight, down, up.reshape(rank, columns))
    out = out.reshape(2 * CHUNKS, steps, block, width).transpose(1, 2, 0, 3)
    return out.reshape(steps, block, columns)


def solution(mesh):
    in_specs = (
        P(None, "groups", "wide"),
        P("wide", None),
        P("wide", None, None),
        P("wide", None, None),
        P(None, "groups", None),
    )
    out_specs = P(None, ("groups", "wide"), None)
    return jax.shard_map(
        functools.partial(shards, mesh.shape["wide"], mesh.shape["groups"]),
        mesh=mesh,
        in_specs=in_specs,
        out_specs=out_specs,
        check_vma=False,
    )
```

```python
import functools

import jax
import jax.numpy as jnp
from jax import lax
from jax.experimental import pallas as pl
from jax.experimental.pallas import tpu as pltpu
from jax.sharding import PartitionSpec as P

CHUNKS = 8
EARLY = 3


def kernel(
    devices,
    groups,
    stages,
    ids_ref,
    acts_given,
    weight_ref,
    down_ref,
    up_ref,
    out_ref,
    acts_ref,
    acts_sib,
    weight_own,
    weight_sib,
    down_all,
    up_pair,
    up_far,
    total,
    low_sum,
    low_part,
    low_got,
    low_all,
    low_mine,
    low_far,
    swap,
    *rest,
):
    sends, gots = rest[:stages], rest[stages : 2 * stages]
    (
        acts_local,
        acts_sem,
        up_sem,
        far_sem,
        weight_send,
        weight_recv,
        weight_local,
        down_send,
        down_recv,
        pass_send,
        low_send,
        low_recv,
        all_send,
        all_recv,
        half_send,
        half_recv,
        swap_send,
        swap_recv,
    ) = rest[2 * stages :]
    me = lax.axis_index("wide")
    group = lax.axis_index("groups")
    core = lax.rem(me, 2)
    chip = me // 2
    sibling = me + 1 - 2 * core
    rows, feats = acts_ref.shape
    rank = up_ref.shape[0]
    chunks, _, width = weight_own.shape
    half_columns = chunks * width
    block = rows // devices

    steps = acts_given.shape[0]
    share = block // steps

    def acts_fetch(i):
        host, step = i // steps, lax.rem(i, steps)
        place = lax.rem(host, 2)
        for s in range(stages):
            place += lax.rem(host // 2 ** (s + 1), 2) * 2 ** (stages - s)
        return pltpu.make_async_copy(
            acts_given.at[step, pl.ds(pl.multiple_of(host * share, share), share)],
            acts_ref.at[pl.ds(pl.multiple_of((place * steps + step) * share, share), share)],
            acts_local.at[i],
        )

    def fetch(i, carry):
        acts_fetch(i).start()
        return carry

    def fetch_end(i, carry):
        acts_fetch(i).wait()
        return carry

    lax.fori_loop(0, devices * steps, fetch, 0)

    barrier = pltpu.get_barrier_semaphore()

    def greet(i, carry):
        pl.semaphore_signal(
            barrier,
            inc=1,
            device_id={"wide": lax.rem(me + i, devices)},
            device_id_type=pl.DeviceIdType.MESH,
        )
        return carry

    lax.fori_loop(1, devices, greet, 0)
    for q in range(1, groups):
        pl.semaphore_signal(
            barrier,
            inc=1,
            device_id={"groups": lax.rem(group + q, groups), "wide": me},
            device_id_type=pl.DeviceIdType.MESH,
        )
    pl.semaphore_wait(barrier, devices + groups - 2)

    def remote(src, dst, send, recv, to):
        return pltpu.make_async_remote_copy(
            src_ref=src,
            dst_ref=dst,
            send_sem=send,
            recv_sem=recv,
            device_id={"wide": to},
            device_id_type=pl.DeviceIdType.MESH,
        )

    def down_copy(to, owner):
        return remote(
            down_ref.at[to],
            down_all.at[pl.ds(pl.multiple_of(owner * rank, rank), rank)],
            down_send.at[to],
            down_recv.at[owner],
            to,
        )

    def pass_copy(owner, q):
        piece = down_all.at[pl.ds(pl.multiple_of(owner * rank, rank), rank)]
        return pltpu.make_async_remote_copy(
            src_ref=piece,
            dst_ref=piece,
            send_sem=pass_send.at[owner * groups + q],
            recv_sem=down_recv.at[owner],
            device_id={"groups": lax.rem(group + q, groups), "wide": me},
            device_id_type=pl.DeviceIdType.MESH,
        )

    def low_copy(to, owner):
        return remote(
            low_part.at[to], low_got.at[owner], low_send.at[to], low_recv.at[owner], to
        )

    def all_copy(to, owner):
        return remote(
            low_all.at[owner], low_all.at[owner], all_send.at[to], all_recv.at[owner], to
        )

    def weight_copy(k):
        start = pl.multiple_of((1 - core) * half_columns + k * width, width)
        return remote(
            weight_ref.at[:, pl.ds(start, width)],
            weight_sib.at[k],
            weight_send.at[k],
            weight_recv.at[k],
            sibling,
        )

    def weight_fetch(k):
        start = pl.multiple_of(core * half_columns + k * width, width)
        return pltpu.make_async_copy(
            weight_ref.at[:, pl.ds(start, width)], weight_own.at[k], weight_local.at[k]
        )

    def each_peer(action):
        def one(i, carry):
            action(lax.rem(me + i, devices))
            return carry

        lax.fori_loop(1, devices, one, 0)

    def each_chunk(action, first=0, end=None):
        def one(k, carry):
            action(k)
            return carry

        lax.fori_loop(first, chunks if end is None else end, one, 0)

    bits = [lax.rem(chip // 2**s, 2) for s in range(stages)]
    partners = [me + 2 ** (s + 1) * (1 - 2 * bits[s]) for s in range(stages)]

    def half_copy(s, k):
        return remote(
            sends[s].at[k],
            gots[s].at[k],
            half_send.at[s * chunks + k],
            half_recv.at[s * chunks + k],
            partners[s],
        )

    half = rows // 2
    away = pl.multiple_of((1 - bits[0]) * half, half)
    kept = pl.multiple_of(bits[0] * half, half)
    early_columns = EARLY * width

    def fetched(peer):
        return lax.rem(me + peer, groups) == group

    own_rank = pl.ds(pl.multiple_of(core * rank, rank), rank)
    acts_copy = remote(acts_ref, acts_sib, acts_sem.at[0], acts_sem.at[1], sibling)
    up_copy = remote(
        up_ref.at[:, pl.ds(pl.multiple_of((1 - core) * half_columns, width), half_columns)],
        up_pair.at[own_rank],
        up_sem.at[0],
        up_sem.at[1],
        sibling,
    )
    up_fetch = pltpu.make_async_copy(
        up_ref.at[:, pl.ds(pl.multiple_of(core * half_columns, width), half_columns)],
        up_pair.at[own_rank],
        up_sem.at[2],
    )
    down_fetch = pltpu.make_async_copy(
        down_ref.at[me],
        down_all.at[pl.ds(pl.multiple_of(me * rank, rank), rank)],
        down_send.at[me],
    )
    each_peer(lambda peer: pl.when(fetched(peer))(lambda: down_copy(peer, me).start()))
    down_fetch.start()
    lax.fori_loop(0, devices * steps, fetch_end, 0)
    acts_copy.start()

    def load(k):
        weight_fetch(k).start()
        weight_copy(k).start()

    each_chunk(load)
    up_copy.start()
    up_fetch.start()

    acts_copy.wait_recv()

    def base(k):
        weight_fetch(k).wait()
        weight_copy(k).wait_recv()
        total[k] = jnp.dot(
            acts_ref[...], weight_own[k], preferred_element_type=jnp.float32
        ) + jnp.dot(acts_sib[...], weight_sib[k], preferred_element_type=jnp.float32)

    def base_early(k):
        base(k)
        sends[0][k] = total[k, pl.ds(away, half)].astype(jnp.bfloat16)
        half_copy(0, k).start()

    far_copy = remote(
        up_pair.at[:, pl.ds(0, early_columns)], up_far, far_sem.at[0], far_sem.at[1], partners[0]
    )
    each_chunk(base_early, 0, EARLY)
    up_fetch.wait()
    up_copy.wait_recv()
    far_copy.start()
    each_chunk(base, EARLY)

    down_fetch.wait()

    def arrive(peer):
        @pl.when(fetched(peer))
        def _():
            down_copy(me, peer).wait_recv()
            for q in range(1, groups):
                pass_copy(peer, q).start()

    def passed(peer):
        @pl.when(jnp.logical_not(fetched(peer)))
        def _():
            down_copy(me, peer).wait_recv()

    each_peer(arrive)
    each_peer(passed)
    odd = (lax.broadcasted_iota(jnp.int32, (rows, 2 * rank), 1) >= rank).astype(jnp.int32)
    number = ids_ref[...] - odd
    low_sum[...] = jnp.zeros_like(low_sum)

    def shrink(j, carry):
        pair = down_all[pl.ds(pl.multiple_of(j * 2 * rank, 2 * rank), 2 * rank)]
        part = lax.dot_general(
            acts_ref[...], pair, (((1,), (1,)), ((), ())), preferred_element_type=jnp.float32
        )
        low_sum[...] += jnp.where(number == 2 * j, part, 0.0)
        return carry

    lax.fori_loop(0, devices // 2, shrink, 0)
    pairs = rows // 2
    left = lax.broadcasted_iota(jnp.int32, (devices, block // 2, 2 * rank), 2) < rank
    both = low_sum[...] + pltpu.roll(low_sum[...], rank, 1)
    both = both.reshape(devices, 2, block // 2, 2 * rank)
    low_part[...] = jnp.where(left, both[:, 0], both[:, 1])
    each_peer(lambda peer: low_copy(peer, me).start())

    def gather(i, value):
        peer = lax.rem(me + i, devices)
        low_copy(me, peer).wait_recv()
        return value + low_got[peer]

    low_all[me] = lax.fori_loop(1, devices, gather, low_part[me]).astype(jnp.bfloat16)
    each_peer(lambda peer: all_copy(peer, me).start())
    each_peer(lambda peer: all_copy(me, peer).wait_recv())
    packed = low_all[...].astype(jnp.float32)
    turned = pltpu.roll(packed.reshape(pairs, 2 * rank), rank, 1).reshape(packed.shape)
    upper, lower = jnp.where(left, packed, turned), jnp.where(left, turned, packed)
    everything = jnp.stack([upper, lower], axis=1).reshape(rows, 2 * rank)
    low_mine[...] = jnp.where(number == 2 * chip, everything, 0.0).astype(jnp.bfloat16)
    low_far[...] = jnp.where(number == 2 * (partners[0] // 2), everything, 0.0).astype(
        jnp.bfloat16
    )

    def delta(k, start):
        return jnp.dot(
            low_mine[pl.ds(start, half)],
            up_pair[:, pl.ds(pl.multiple_of(k * width, width), width)],
            preferred_element_type=jnp.float32,
        )

    def first(k):
        sends[0][k] = (total[k, pl.ds(away, half)] + delta(k, away)).astype(jnp.bfloat16)
        half_copy(0, k).start()

    def second(k):
        total[k, pl.ds(kept, half)] += delta(k, kept)

    def second_far(k):
        total[k, pl.ds(kept, half)] += jnp.dot(
            low_far[pl.ds(kept, half)],
            up_far[:, pl.ds(pl.multiple_of(k * width, width), width)],
            preferred_element_type=jnp.float32,
        )

    each_chunk(first, EARLY)
    far_copy.wait_recv()

    def swap_copy(k):
        return remote(
            swap.at[k],
            out_ref.at[core * chunks + k],
            swap_send.at[k],
            swap_recv.at[k],
            sibling,
        )

    def finish(s, k, offset, size):
        half_copy(s, k).wait_recv()
        small = size // 2
        last = s == stages - 1
        bit = core if last else bits[s + 1]
        there = pl.multiple_of((1 - bit) * small, small)
        here = pl.multiple_of(bit * small, small)
        away = total[k, pl.ds(pl.multiple_of(offset + there, small), small)] + gots[s][
            k, pl.ds(there, small)
        ].astype(jnp.float32)
        if last:
            swap[k] = away.astype(jnp.bfloat16)
            swap_copy(k).start()
        else:
            sends[s + 1][k] = away.astype(jnp.bfloat16)
            half_copy(s + 1, k).start()
        mine = pl.ds(pl.multiple_of(offset + here, small), small)
        value = total[k, mine] + gots[s][k, pl.ds(here, small)].astype(jnp.float32)
        if last:
            out_ref[core * chunks + k] = value.astype(jnp.bfloat16)
        else:
            total[k, mine] = value

    offsets, sizes = [kept], [half]
    for s in range(1, stages):
        sizes.append(sizes[-1] // 2)
        offsets.append(offsets[-1] + bits[s] * sizes[-1])

    def step(t, carry):
        pl.when(t < chunks)(lambda: second(t))
        pl.when(t < EARLY)(lambda: second_far(t))
        for s in range(stages):

            @pl.when((t >= s) & (t - s < chunks))
            def _():
                finish(s, t - s, offsets[s], sizes[s])

        return carry

    lax.fori_loop(0, chunks + stages - 1, step, 0)

    other = 1 - core

    def close(k):
        remote(
            swap.at[k],
            out_ref.at[other * chunks + k],
            swap_send.at[k],
            swap_recv.at[k],
            sibling,
        ).wait_recv()
        swap_copy(k).wait_send()
        weight_copy(k).wait_send()
        for s in range(stages):
            half_copy(s, k).wait_send()

    each_chunk(close)

    def close_peer(peer):
        @pl.when(fetched(peer))
        def _():
            down_copy(peer, me).wait_send()
            for q in range(1, groups):
                pass_copy(peer, q).wait_send()

        low_copy(peer, me).wait_send()
        all_copy(peer, me).wait_send()

    each_peer(close_peer)
    acts_copy.wait_send()
    up_copy.wait_send()
    far_copy.wait_send()


def shards(devices, groups, acts, weight, down, up, numbers):
    steps, rows, feats = acts.shape
    rank, columns = up.shape[1:]
    chips = devices // 2
    stages = chips.bit_length() - 1
    block = rows // devices
    total_rows = steps * rows
    width = columns // 2 // CHUNKS
    order = tuple(range(stages, 0, -1)) + (stages + 1, 0, stages + 2, stages + 3)

    def arranged(array):
        array = array.reshape((steps,) + (2,) * stages + (2, block, array.shape[-1]))
        return array.transpose(order).reshape(total_rows, array.shape[-1])

    down = down.reshape(devices, feats, rank).swapaxes(1, 2)
    bf16, f32 = jnp.bfloat16, jnp.float32
    low_block = (devices, total_rows // devices // 2, 2 * rank)
    halves = [(CHUNKS, total_rows >> (s + 1), width) for s in range(stages)]
    dma = pltpu.SemaphoreType.DMA
    out = pl.pallas_call(
        functools.partial(kernel, devices, groups, stages),
        out_shape=jax.ShapeDtypeStruct((2 * CHUNKS, steps * block, width), bf16),
        in_specs=[
            pl.BlockSpec(memory_space=pltpu.VMEM),
            pl.BlockSpec(memory_space=pl.ANY),
            pl.BlockSpec(memory_space=pl.ANY),
            pl.BlockSpec(memory_space=pl.ANY),
            pl.BlockSpec(memory_space=pl.ANY),
        ],
        out_specs=pl.BlockSpec(memory_space=pltpu.VMEM),
        scratch_shapes=[
            pltpu.VMEM((total_rows, feats), bf16),
            pltpu.VMEM((total_rows, feats), bf16),
            pltpu.VMEM((CHUNKS, feats, width), bf16),
            pltpu.VMEM((CHUNKS, feats, width), bf16),
            pltpu.VMEM((devices * rank, feats), bf16),
            pltpu.VMEM((2 * rank, columns // 2), bf16),
            pltpu.VMEM((2 * rank, EARLY * width), bf16),
            pltpu.VMEM((CHUNKS, total_rows, width), f32),
            pltpu.VMEM((total_rows, 2 * rank), f32),
            pltpu.VMEM(low_block, f32),
            pltpu.VMEM(low_block, f32),
            pltpu.VMEM(low_block, bf16),
            pltpu.VMEM((total_rows, 2 * rank), bf16),
            pltpu.VMEM((total_rows, 2 * rank), bf16),
            pltpu.VMEM((CHUNKS, steps * block, width), bf16),
        ]
        + [pltpu.VMEM(shape, bf16) for shape in halves]
        + [pltpu.VMEM(shape, bf16) for shape in halves]
        + [dma((steps * devices,)), dma((2,)), dma((3,)), dma((2,))]
        + [dma((CHUNKS,))] * 3
        + [dma((devices,))] * 2
        + [dma((devices * groups,))]
        + [dma((devices,))] * 4
        + [dma((stages * CHUNKS,))] * 2
        + [dma((CHUNKS,))] * 2,
        compiler_params=pltpu.CompilerParams(
            collective_id=0, has_side_effects=True, vmem_limit_bytes=58 * 1024 * 1024
        ),
    )(arranged(numbers), acts, weight, down, up.reshape(rank, columns))
    out = out.reshape(2 * CHUNKS, steps, block, width).transpose(1, 2, 0, 3)
    return out.reshape(steps, block, columns)


def solution(mesh):
    in_specs = (
        P(None, "groups", "wide"),
        P("wide", None),
        P("wide", None, None),
        P("wide", None, None),
        P(None, "groups", None),
    )
    out_specs = P(None, ("groups", "wide"), None)
    return jax.shard_map(
        functools.partial(shards, mesh.shape["wide"], mesh.shape["groups"]),
        mesh=mesh,
        in_specs=in_specs,
        out_specs=out_specs,
        check_vma=False,
    )
```
